32 devices in a mesh: case: 2 (over x), space: 16 (over z, y, core).
Axes of the slice: x: 2, y: 2, z: 4, core: 2. Of those that a mesh axis runs over, the one named last changes fastest.
Arguments:
- snapshots: float32 [1024, 8192], P('space', 'case'), parts along dimension 1, may hold values from -6 to 6
- weights: float32 [8192], P(('case', 'space')), parts along dimension 0, may hold values from 0.25 to 4
- counts: int32 [32], P(('case', 'space')), parts along dimension 0, may hold values from 85 to 256, as said below
- starts: int32 [8], replicated, may hold values from 0 to 768, as said below
Outputs:
- modes: bfloat16 [2, 8, 129, 8192], P(None, None, None, ('case', 'space')), parts along dimension 3
- r_factor: float32 [2, 258, 8, 8], P(None, 'case'), parts along dimension 1
The draws below stay inside these ranges and needn't reach their ends.
There are 2 independent parts, one for each index of `case`. The reference program is written for one: setup_inputs(seed, part) draws one part's arguments, and reference() takes and returns one part's arrays. A program takes and returns all parts, laid end to end along the dimension named above; an argument that names none is the same for every part. Nothing has to cross between parts.
Inputs may be any that keep to these rules, and one draw needn't show every extreme that they name: The first block starts at 0 and the last at 768. The live points of a shard are its first counts slots; some shard is full.
All inputs are finite; a program needn't handle non-finite values.
Results may differ from the reference program's by a relative error of at most 0.001.
Values sent between devices are 32-bit elements; how exact they have to be, the bound alone decides.
A program may use at most 256 MiB of HBM per device.

```python
import math
import jax
import jax.numpy as jnp
from jax import lax

NFFT = 256
NBLK = 8
NT = 1024
P_DEV = 256
SHARDS = 16
POINTS = 4096


def draw_counts(key, part):
    lowest = P_DEV // 3
    shard_ids = jnp.arange(SHARDS, dtype=jnp.int32)
    ramp = lowest + (P_DEV - lowest) * shard_ids // (SHARDS - 1)
    jitter = jax.random.randint(key, (SHARDS,), 0, P_DEV // 16 + 1, dtype=jnp.int32)
    values = jnp.maximum(ramp - jitter, lowest)
    values = values.at[SHARDS - 1].set(P_DEV)
    return values.astype(jnp.int32)


def draw_starts(key, part):
    span = NT - NFFT
    spacing = span // (NBLK - 1)
    block_ids = jnp.arange(NBLK, dtype=jnp.int32)
    jitter = jax.random.randint(key, (NBLK,), 0, spacing // 2 + 1, dtype=jnp.int32)
    values = jnp.clip(block_ids * spacing - jitter, 0, span)
    values = values.at[NBLK - 1].set(span)
    return values.astype(jnp.int32)


def steps_of(own_key, extent, pieces, low, largest):
    def one(position, parts):
        draws = jax.random.uniform(jax.random.fold_in(jax.random.fold_in(own_key, 6), position), (parts,), jnp.float32, low / len(pieces), largest / len(pieces))
        return jnp.repeat(jnp.exp(draws), extent[position] // parts).reshape((-1,) + (1,) * (len(extent) - position - 1))

    loudness = one(*pieces[0])
    for cut in pieces[1:]:
        loudness = loudness * one(*cut)
    return loudness


def noise(own_key, extent, spread, limit, split=(), held_as=jnp.bfloat16):
    array = spread * jax.random.normal(own_key, extent, jnp.float32)
    if split:
        array = array * steps_of(own_key, extent, split, -0.22, 0.18)
    return jnp.clip(array, -limit, limit).astype(held_as)


def setup_inputs(seed: int = 0, part: int = 0) -> dict:
    keys = jax.random.split(jax.random.key(seed), 5)
    part_keys = jax.random.split(jax.random.fold_in(keys[4], part), 5)
    snapshots = noise(part_keys[0], (NT, POINTS), 1.0, 6.0, ((0, 16),), jnp.float32)
    weights = jnp.clip(jnp.exp(math.log(4.0) - 2.7725887 * jax.random.uniform(part_keys[1], (POINTS,), jnp.float32) ** steps_of(part_keys[1], (POINTS,), ((0, 16),), -0.2, 0.2)), 0.25, 4.0)
    counts = draw_counts(jax.random.fold_in(jax.random.fold_in(keys[4], part), 71), part)
    starts = draw_starts(jax.random.fold_in(keys[4], 71), part)
    return {"snapshots": snapshots, "weights": weights, "counts": counts, "starts": starts}


def window_table():
    moment = jnp.arange(NFFT, dtype=jnp.int32)
    harmonic = jnp.arange(NFFT // 2 + 1, dtype=jnp.int32)
    hann_window = 0.5 - 0.5 * jnp.cos(2.0 * jnp.pi * moment.astype(jnp.float32) / NFFT)
    norm_scale = 1.0 / jnp.sqrt(jnp.sum(hann_window * hann_window))
    folded = harmonic[:, None] * moment[None, :] % NFFT
    angle_table = 2.0 * jnp.pi * folded.astype(jnp.float32) / NFFT
    cosine = jnp.cos(angle_table) * (hann_window * norm_scale)[None, :]
    sine = -jnp.sin(angle_table) * (hann_window * norm_scale)[None, :]
    return jnp.concatenate([cosine, sine], axis=0)

def realize(record, starts, dft_table):
    centered = record - lax.optimization_barrier(jnp.mean(record, axis=0, keepdims=True))
    outputs = []
    for block_id in range(NBLK):
        segment = lax.dynamic_slice_in_dim(centered, starts[block_id].astype(jnp.int32), NFFT, 0)
        outputs.append(jnp.dot(dft_table, segment, precision=lax.Precision.HIGHEST, preferred_element_type=jnp.float32))
    return jnp.stack(outputs, axis=0)

def gram_parts(realized, live_area):
    half_f = realized.shape[1] // 2
    real_part = realized[:, :half_f]
    imag_part = realized[:, half_f:]
    weighted_re = real_part * live_area
    weighted_im = imag_part * live_area
    high = lax.Precision.HIGHEST
    gram_re = jnp.einsum('kfp,lfp->fkl', weighted_re, real_part, precision=high) + jnp.einsum('kfp,lfp->fkl', weighted_im, imag_part, precision=high)
    gram_im = jnp.einsum('kfp,lfp->fkl', weighted_re, imag_part, precision=high) - jnp.einsum('kfp,lfp->fkl', weighted_im, real_part, precision=high)
    return (gram_re, gram_im)

def stack_entries(entries):
    return jnp.stack([jnp.stack(row_list, axis=1) for row_list in entries], axis=1)

def cholesky_upper(gram_re, gram_im):
    blocks_n = gram_re.shape[-1]
    zeros_f = jnp.zeros_like(gram_re[:, 0, 0])
    fac_re = [[zeros_f for column in range(blocks_n)] for row in range(blocks_n)]
    fac_im = [[zeros_f for column in range(blocks_n)] for row in range(blocks_n)]
    for row in range(blocks_n):
        pivot = gram_re[:, row, row]
        for upper in range(row):
            pivot = pivot - fac_re[upper][row] * fac_re[upper][row] - fac_im[upper][row] * fac_im[upper][row]
        diagonal = jnp.sqrt(pivot)
        fac_re[row][row] = diagonal
        for column in range(row + 1, blocks_n):
            sum_re = gram_re[:, row, column]
            sum_im = gram_im[:, row, column]
            for upper in range(row):
                sum_re = sum_re - (fac_re[upper][row] * fac_re[upper][column] + fac_im[upper][row] * fac_im[upper][column])
                sum_im = sum_im - (fac_re[upper][row] * fac_im[upper][column] - fac_im[upper][row] * fac_re[upper][column])
            fac_re[row][column] = sum_re / diagonal
            fac_im[row][column] = sum_im / diagonal
    return (stack_entries(fac_re), stack_entries(fac_im))

def invert_upper(fac_re, fac_im):
    blocks_n = fac_re.shape[-1]
    zeros_f = jnp.zeros_like(fac_re[:, 0, 0])
    inv_re = [[zeros_f for column in range(blocks_n)] for row in range(blocks_n)]
    inv_im = [[zeros_f for column in range(blocks_n)] for row in range(blocks_n)]
    for column in range(blocks_n):
        inv_re[column][column] = 1.0 / fac_re[:, column, column]
        for row in range(column - 1, -1, -1):
            sum_re = zeros_f
            sum_im = zeros_f
            for middle in range(row + 1, column + 1):
                sum_re = sum_re + fac_re[:, row, middle] * inv_re[middle][column] - fac_im[:, row, middle] * inv_im[middle][column]
                sum_im = sum_im + fac_re[:, row, middle] * inv_im[middle][column] + fac_im[:, row, middle] * inv_re[middle][column]
            pivot = fac_re[:, row, row]
            inv_re[row][column] = -sum_re / pivot
            inv_im[row][column] = -sum_im / pivot
    return (stack_entries(inv_re), stack_entries(inv_im))

def modes_from(realized, inv_re, inv_im, live_mask):
    half_f = realized.shape[1] // 2
    real_part = realized[:, :half_f]
    imag_part = realized[:, half_f:]
    high = lax.Precision.HIGHEST
    basis_re = jnp.einsum('kfp,fkl->lfp', real_part, inv_re, precision=high) - jnp.einsum('kfp,fkl->lfp', imag_part, inv_im, precision=high)
    basis_im = jnp.einsum('kfp,fkl->lfp', real_part, inv_im, precision=high) + jnp.einsum('kfp,fkl->lfp', imag_part, inv_re, precision=high)
    return jnp.stack([basis_re * live_mask, basis_im * live_mask], axis=0).astype(jnp.bfloat16)

def reference(snapshots, weights, counts, starts):
    dft_table = window_table()

    def one_shard(shard_id):
        record = lax.dynamic_slice_in_dim(snapshots, shard_id * P_DEV, P_DEV, 1)
        realized = realize(record, starts, dft_table)
        live_mask = (jnp.arange(P_DEV, dtype=jnp.int32) < counts[shard_id]).astype(jnp.float32)
        live_area = lax.dynamic_slice_in_dim(weights, shard_id * P_DEV, P_DEV, 0) * live_mask
        gram_re, gram_im = gram_parts(realized, live_area)
        return (realized, live_mask, gram_re, gram_im, jnp.sum(live_area))
    realized_all, live_all, gram_re_all, gram_im_all, area_all = lax.map(one_shard, jnp.arange(SHARDS, dtype=jnp.int32))
    area_total = jnp.sum(area_all)
    gram_re = lax.optimization_barrier(jnp.sum(gram_re_all, axis=0)) / area_total
    gram_im = lax.optimization_barrier(jnp.sum(gram_im_all, axis=0)) / area_total
    fac_re, fac_im = cholesky_upper(gram_re, gram_im)
    inv_re, inv_im = invert_upper(fac_re, fac_im)

    def shard_modes(pair):
        return modes_from(pair[0], inv_re, inv_im, pair[1])
    modes_all = lax.map(shard_modes, (realized_all, live_all))
    modes = jnp.transpose(modes_all, (1, 2, 3, 0, 4)).reshape(2, NBLK, NFFT // 2 + 1, SHARDS * P_DEV)
    return (modes, jnp.stack([fac_re, fac_im], axis=0))
```

```python
import functools

import jax
import jax.numpy as jnp
import numpy as np
from jax import lax
from jax.experimental import pallas as pl
from jax.experimental.pallas import tpu as pltpu
from jax.sharding import PartitionSpec as P

NFFT = 256
NBLK = 8
NFREQ = NFFT // 2 + 1
FROWS = 136
LANES = 128
SLOT = 72


def window_table():
    moment = np.arange(NFFT)
    harmonic = np.arange(NFREQ)
    hann = 0.5 - 0.5 * np.cos(2.0 * np.pi * moment / NFFT)
    scale = 1.0 / np.sqrt(np.sum(hann * hann))
    angle = 2.0 * np.pi * (harmonic[:, None] * moment[None, :] % NFFT) / NFFT
    table = np.zeros((2 * FROWS, NFFT))
    table[:NFREQ] = np.cos(angle) * hann * scale
    table[FROWS : FROWS + NFREQ] = -np.sin(angle) * hann * scale
    table = table.astype(np.float32)
    high = table.astype(jnp.bfloat16)
    low = (table - high.astype(np.float32)).astype(jnp.bfloat16)
    both = np.concatenate([high, low], axis=0)
    return np.stack([np.roll(both, turn, axis=1) for turn in range(8)])


def kernel(
    n,
    starts_ref,
    live_ref,
    snap_ref,
    table_hbm,
    modes_ref,
    factor_ref,
    rec,
    table,
    real,
    gram,
    slots,
    coef,
    own_sem,
    table_sem,
    send_a,
    recv_a,
    send_g,
    recv_g,
):
    me = lax.axis_index("space")
    rows = snap_ref.shape[0]
    points = snap_ref.shape[1] // n
    mesh_type = pl.DeviceIdType.MESH

    def peer(step):
        return lax.rem(me + step, n)

    barrier = pltpu.get_barrier_semaphore()

    def greet(step, carry):
        pl.semaphore_signal(
            barrier, inc=1, device_id={"space": peer(step)}, device_id_type=mesh_type
        )
        return carry

    lax.fori_loop(1, n, greet, 0)
    my_rows = pl.ds(pl.multiple_of(me * rows, 8), rows)

    def columns(shard):
        return pl.ds(pl.multiple_of(shard * points, LANES), points)

    own = pltpu.make_async_copy(snap_ref.at[:, columns(me)], rec.at[my_rows, :], own_sem)
    own.start()
    fetch = pltpu.make_async_copy(table_hbm, table, table_sem)
    fetch.start()
    pl.semaphore_wait(barrier, n - 1)

    def block_copy(step):
        dest = peer(step)
        return pltpu.make_async_remote_copy(
            src_ref=snap_ref.at[:, columns(dest)],
            dst_ref=rec.at[my_rows, :],
            send_sem=send_a.at[step],
            recv_sem=recv_a.at[step],
            device_id={"space": dest},
            device_id_type=mesh_type,
        )

    def gram_copy(step):
        return pltpu.make_async_remote_copy(
            src_ref=slots.at[me],
            dst_ref=slots.at[me],
            send_sem=send_g.at[step],
            recv_sem=recv_g.at[step],
            device_id={"space": peer(step)},
            device_id_type=mesh_type,
        )

    def start_all(make):
        def body(step, carry):
            make(step).start()
            return carry

        lax.fori_loop(1, n, body, 0)

    def wait_all(make, sending):
        def body(step, carry):
            if sending:
                make(step).wait_send()
            else:
                make(step).wait_recv()
            return carry

        lax.fori_loop(1, n, body, 0)

    start_all(block_copy)
    live = live_ref[0:1, :]
    area = live_ref[1:2, :]
    own.wait()
    fetch.wait()
    wait_all(block_copy, False)

    record_rows = rows * n
    rec[record_rows : record_rows + 8, :] = jnp.zeros((8, points), jnp.float32)

    def add_rows(chunk, total):
        return total + rec[pl.ds(pl.multiple_of(chunk * 64, 64), 64), :]

    sums = lax.fori_loop(0, record_rows // 64, add_rows, jnp.zeros((64, points), jnp.float32))
    mean = jnp.sum(sums, axis=0, keepdims=True) * (1.0 / record_rows)

    early = lax.broadcasted_iota(jnp.int32, (8, points), 0)

    def transform(block, carry):
        start = starts_ref[block]
        base = lax.div(start, 8) * 8
        shift = start - base
        wrapped = jnp.where(early < shift, rec[pl.ds(base + NFFT, 8), :], rec[pl.ds(base, 8), :])
        segment = jnp.concatenate([wrapped, rec[pl.ds(base + 8, NFFT - 8), :]], axis=0) - mean
        seg_high = segment.astype(jnp.bfloat16)
        seg_low = (segment - seg_high.astype(jnp.float32)).astype(jnp.bfloat16)
        high = table[shift, 0 : 2 * FROWS, :]
        low = table[shift, 2 * FROWS : 4 * FROWS, :]
        dot = functools.partial(jnp.dot, preferred_element_type=jnp.float32)
        real[block] = dot(high, seg_high) + (dot(high, seg_low) + dot(low, seg_high))
        return carry

    lax.fori_loop(0, NBLK, transform, 0)

    lane = lax.broadcasted_iota(jnp.int32, (8, LANES), 1)

    def gram_tile(tile, carry):
        re_rows = pl.ds(pl.multiple_of(tile * 8, 8), 8)
        im_rows = pl.ds(pl.multiple_of(FROWS + tile * 8, 8), 8)
        packed = jnp.zeros((8, LANES), jnp.float32)
        q_re = [real[k, re_rows, :] for k in range(NBLK)]
        q_im = [real[k, im_rows, :] for k in range(NBLK)]
        for k in range(NBLK):
            w_re = q_re[k] * area
            w_im = q_im[k] * area
            for l in range(k, NBLK):
                entry = jnp.sum(w_re * q_re[l] + w_im * q_im[l], axis=1, keepdims=True)
                packed = jnp.where(lane == k * 8 + l, entry, packed)
                if l > k:
                    entry = jnp.sum(w_re * q_im[l] - w_im * q_re[l], axis=1, keepdims=True)
                    packed = jnp.where(lane == (7 - k) * 8 + l - k - 1, entry, packed)
        gram[re_rows, :] = packed
        return carry

    lax.fori_loop(0, FROWS // 8, gram_tile, 0)
    local_area = jnp.sum(area, axis=1, keepdims=True)
    sub = lax.broadcasted_iota(jnp.int32, (8, LANES), 0)
    slots[me, 0:64, :] = jnp.transpose(gram[0:LANES, :])[0:64, :]
    slots[me, 64:SLOT, :] = jnp.where(sub == 1, local_area, gram[LANES:FROWS, :])
    start_all(gram_copy)
    wait_all(gram_copy, False)

    def add_slot(shard, total):
        return total + slots[shard]

    summed = lax.fori_loop(1, n, add_slot, slots[0])
    tail = summed[64:SLOT, :]
    per_area = 1.0 / tail[1:2, :]
    tail_t = jnp.transpose(jnp.concatenate([tail * per_area] * (LANES // 8), axis=0))
    summed = jnp.concatenate([summed[0:64, :] * per_area, tail_t[0:64, :]], axis=1)

    column = lax.broadcasted_iota(jnp.int32, (NBLK, 2 * LANES), 0)
    valid = lax.broadcasted_iota(jnp.int32, (NBLK, 2 * LANES), 1) < NFREQ
    a_re = []
    a_im = []
    for i in range(NBLK):
        unit = jnp.where(column == i, 1.0, 0.0)
        a_re.append(jnp.where(valid, summed[8 * i : 8 * i + 8, :], unit))
        part = summed[8 * (7 - i) : 8 * (7 - i) + 8, :]
        part = pltpu.roll(part, i + 1, 0) if i < NBLK - 1 else part
        a_im.append(jnp.where(valid & (column > i), part, 0.0))
    r_re = []
    r_im = []
    inv_diag = []
    for i in range(NBLK):
        scale = 1.0 / jnp.sqrt(a_re[i][i : i + 1, :])
        inv_diag.append(scale)
        r_re.append(jnp.where(column >= i, a_re[i] * scale, 0.0))
        r_im.append(jnp.where(column > i, a_im[i] * scale, 0.0))
        for k in range(i + 1, NBLK):
            c_re = r_re[i][k : k + 1, :]
            c_im = r_im[i][k : k + 1, :]
            a_re[k] = a_re[k] - (c_re * r_re[i] + c_im * r_im[i])
            a_im[k] = a_im[k] - (c_re * r_im[i] - c_im * r_re[i])
    x_re = [None] * NBLK
    x_im = [None] * NBLK
    for i in range(NBLK - 1, -1, -1):
        sum_re = jnp.where(column == i, 1.0, 0.0)
        sum_im = jnp.zeros((NBLK, 2 * LANES), jnp.float32)
        for m in range(i + 1, NBLK):
            c_re = r_re[i][m : m + 1, :]
            c_im = r_im[i][m : m + 1, :]
            sum_re = sum_re - (c_re * x_re[m] - c_im * x_im[m])
            sum_im = sum_im - (c_re * x_im[m] + c_im * x_re[m])
        x_re[i] = sum_re * inv_diag[i]
        x_im[i] = sum_im * inv_diag[i]

    def by_frequency(parts_re, parts_im):
        stacked = jnp.concatenate(parts_re + parts_im, axis=0)
        head = jnp.transpose(stacked[:, 0:LANES])
        end = jnp.transpose(stacked[:, LANES : 2 * LANES])
        return head, end[0:8, :]

    head, end = by_frequency(x_re, x_im)
    coef[0:LANES, :] = head
    coef[LANES:FROWS, :] = end
    head, end = by_frequency(r_re, r_im)
    factor_ref[0:LANES, :] = head
    factor_ref[LANES:FROWS, :] = end

    def mode_rows(first, count, store):
        re_rows = pl.ds(first, count)
        im_rows = pl.ds(FROWS + first, count)
        c = coef[re_rows, :]
        for l in range(NBLK):
            out_re = jnp.zeros((count, points), jnp.float32)
            out_im = jnp.zeros((count, points), jnp.float32)
            for k in range(l + 1):
                q_re = real[k, re_rows, :]
                q_im = real[k, im_rows, :]
                c_re = c[:, k * 8 + l : k * 8 + l + 1]
                out_re = out_re + q_re * c_re
                out_im = out_im + q_im * c_re
                if k < l:
                    c_im = c[:, 64 + k * 8 + l : 64 + k * 8 + l + 1]
                    out_re = out_re - q_im * c_im
                    out_im = out_im + q_re * c_im
            store(0, l, (out_re * live).astype(jnp.bfloat16))
            store(1, l, (out_im * live).astype(jnp.bfloat16))

    def mode_tile(tile, carry):
        first = pl.multiple_of(tile * 16, 16)

        def store(part, l, value):
            modes_ref[part, l, pl.ds(first, 16), :] = value

        mode_rows(first, 16, store)
        return carry

    lax.fori_loop(0, LANES // 16, mode_tile, 0)

    def store_tail(part, l, value):
        modes_ref[part, l, LANES:NFREQ, :] = value[0 : NFREQ - LANES, :]

    mode_rows(LANES, 8, store_tail)
    wait_all(block_copy, True)
    wait_all(gram_copy, True)


def per_device(snapshots, weights, counts, starts):
    n = lax.axis_size("space")
    rows, width = snapshots.shape
    points = width // n
    live = (jnp.arange(points, dtype=jnp.int32) < counts[0]).astype(jnp.float32)
    vmem = pl.BlockSpec(memory_space=pltpu.VMEM)
    smem = pl.BlockSpec(memory_space=pltpu.SMEM)
    anywhere = pl.BlockSpec(memory_space=pl.ANY)
    dma = pltpu.SemaphoreType.DMA
    modes, factor = pl.pallas_call(
        functools.partial(kernel, n),
        out_shape=(
            jax.ShapeDtypeStruct((2, NBLK, NFREQ, points), jnp.bfloat16),
            jax.ShapeDtypeStruct((FROWS, LANES), jnp.float32),
        ),
        in_specs=[smem, vmem, anywhere, anywhere],
        out_specs=(vmem, vmem),
        scratch_shapes=[
            pltpu.VMEM((rows * n + 8, points), jnp.float32),
            pltpu.VMEM((8, 4 * FROWS, NFFT), jnp.bfloat16),
            pltpu.VMEM((NBLK, 2 * FROWS, points), jnp.float32),
            pltpu.VMEM((FROWS, LANES), jnp.float32),
            pltpu.VMEM((n, SLOT, LANES), jnp.float32),
            pltpu.VMEM((FROWS, LANES), jnp.float32),
            dma,
            dma,
            dma((n,)),
            dma((n,)),
            dma((n,)),
            dma((n,)),
        ],
        compiler_params=pltpu.CompilerParams(
            collective_id=0, has_side_effects=True, vmem_limit_bytes=40 * 2**20
        ),
    )(starts, jnp.stack([live, weights * live]), snapshots, jnp.asarray(window_table()))
    factor = factor[:NFREQ].reshape(NFREQ, 2, NBLK, NBLK)
    return (modes, jnp.moveaxis(factor, 1, 0))


def solution(mesh):
    in_specs = (P("space", "case"), P(("case", "space")), P(("case", "space")), P())
    out_specs = (P(None, None, None, ("case", "space")), P(None, "case", None, None))
    return jax.shard_map(
        per_device, mesh=mesh, in_specs=in_specs, out_specs=out_specs, check_vma=False
    )
```

```python
import functools

import jax
import jax.numpy as jnp
import numpy as np
from jax import lax
from jax.experimental import pallas as pl
from jax.experimental.pallas import tpu as pltpu
from jax.sharding import PartitionSpec as P

NFFT = 256
NBLK = 8
NFREQ = NFFT // 2 + 1
FROWS = 136
LANES = 128
SLOT = 72


def window_table():
    moment = np.arange(NFFT)
    harmonic = np.arange(NFREQ)
    hann = 0.5 - 0.5 * np.cos(2.0 * np.pi * moment / NFFT)
    scale = 1.0 / np.sqrt(np.sum(hann * hann))
    angle = 2.0 * np.pi * (harmonic[:, None] * moment[None, :] % NFFT) / NFFT
    table = np.zeros((2 * FROWS, NFFT))
    table[:NFREQ] = np.cos(angle) * hann * scale
    table[FROWS : FROWS + NFREQ] = -np.sin(angle) * hann * scale
    table = table.astype(np.float32)
    high = table.astype(jnp.bfloat16)
    low = (table - high.astype(np.float32)).astype(jnp.bfloat16)
    both = np.concatenate([high, low], axis=0)
    return np.stack([np.roll(both, turn, axis=1) for turn in range(8)])


def stages_of(n):
    return [(1, 2), (2, 2), (4, n // 4)]


def kernel(
    n,
    starts_ref,
    counts_ref,
    weights_ref,
    snap_ref,
    table_hbm,
    modes_ref,
    factor_ref,
    rec,
    table,
    real,
    gram,
    slots,
    coef,
    send_sem,
    recv_sem,
    own_sem,
    table_sem,
    block_send,
    block_recv,
):
    me = lax.axis_index("space")
    rows = snap_ref.shape[0]
    points = snap_ref.shape[1] // n
    record_rows = rows * n
    mesh_type = pl.DeviceIdType.MESH

    def peer(stride, size, step):
        place = lax.rem(lax.div(me, stride), size)
        return me + (lax.rem(place + step, size) - place) * stride

    barrier = pltpu.get_barrier_semaphore()

    def greet(step, carry):
        pl.semaphore_signal(
            barrier,
            inc=1,
            device_id={"space": lax.rem(me + step, n)},
            device_id_type=mesh_type,
        )
        return carry

    lax.fori_loop(1, n, greet, 0)

    def rows_of(shard):
        return pl.ds(pl.multiple_of(shard * rows, 8), rows)

    def columns(shard):
        return pl.ds(pl.multiple_of(shard * points, LANES), points)

    def block_copy(turn):
        step = 1 + lax.rem(turn + n // 2 - 1, n - 1)
        dest = lax.rem(me + step, n)
        return pltpu.make_async_remote_copy(
            src_ref=snap_ref.at[:, columns(dest)],
            dst_ref=rec.at[rows_of(me), :],
            send_sem=block_send.at[step],
            recv_sem=block_recv.at[step],
            device_id={"space": dest},
            device_id_type=mesh_type,
        )

    own = pltpu.make_async_copy(snap_ref.at[:, columns(me)], rec.at[rows_of(me), :], own_sem)
    fetch = pltpu.make_async_copy(table_hbm, table, table_sem)
    pl.semaphore_wait(barrier, n - 1)

    def send_block(turn, carry):
        block_copy(turn).start()
        return carry

    lax.fori_loop(0, n - 1, send_block, 0)
    own.start()
    fetch.start()
    live = (lax.broadcasted_iota(jnp.int32, (1, points), 1) < counts_ref[0]).astype(jnp.float32)
    area = weights_ref[...] * live

    own.wait()

    def take_block(turn, total):
        step = 1 + turn
        pltpu.make_async_remote_copy(
            src_ref=snap_ref.at[:, columns(me)],
            dst_ref=rec.at[rows_of(me), :],
            send_sem=block_send.at[step],
            recv_sem=block_recv.at[step],
            device_id={"space": lax.rem(me + step, n)},
            device_id_type=mesh_type,
        ).wait_recv()
        return total + rec[rows_of(lax.rem(me + n - step, n)), :]

    sums = lax.fori_loop(0, n - 1, take_block, rec[rows_of(me), :])
    mean = jnp.sum(sums, axis=0, keepdims=True) * (1.0 / record_rows)
    rec[record_rows : record_rows + 8, :] = jnp.zeros((8, points), jnp.float32)
    fetch.wait()

    early = lax.broadcasted_iota(jnp.int32, (8, points), 0)

    def transform(block, carry):
        start = starts_ref[block]
        base = lax.div(start, 8) * 8
        shift = start - base
        wrapped = jnp.where(early < shift, rec[pl.ds(base + NFFT, 8), :], rec[pl.ds(base, 8), :])
        segment = jnp.concatenate([wrapped, rec[pl.ds(base + 8, NFFT - 8), :]], axis=0) - mean
        seg_high = segment.astype(jnp.bfloat16)
        seg_low = (segment - seg_high.astype(jnp.float32)).astype(jnp.bfloat16)
        high = table[shift, 0 : 2 * FROWS, :]
        low = table[shift, 2 * FROWS : 4 * FROWS, :]
        dot = functools.partial(jnp.dot, preferred_element_type=jnp.float32)
        real[block] = dot(high, seg_high) + (dot(high, seg_low) + dot(low, seg_high))
        return carry

    lax.fori_loop(0, NBLK, transform, 0)

    lane = lax.broadcasted_iota(jnp.int32, (8, LANES), 1)

    def gram_tile(tile, carry):
        re_rows = pl.ds(pl.multiple_of(tile * 8, 8), 8)
        im_rows = pl.ds(pl.multiple_of(FROWS + tile * 8, 8), 8)
        packed = jnp.zeros((8, LANES), jnp.float32)
        q_re = [real[k, re_rows, :] for k in range(NBLK)]
        q_im = [real[k, im_rows, :] for k in range(NBLK)]
        for k in range(NBLK):
            w_re = q_re[k] * area
            w_im = q_im[k] * area
            for l in range(k, NBLK):
                entry = jnp.sum(w_re * q_re[l] + w_im * q_im[l], axis=1, keepdims=True)
                packed = jnp.where(lane == k * 8 + l, entry, packed)
                if l > k:
                    entry = jnp.sum(w_re * q_im[l] - w_im * q_re[l], axis=1, keepdims=True)
                    packed = jnp.where(lane == (7 - k) * 8 + l - k - 1, entry, packed)
        gram[re_rows, :] = packed
        return carry

    lax.fori_loop(0, FROWS // 8, gram_tile, 0)
    local_area = jnp.sum(area, axis=1, keepdims=True)
    sub = lax.broadcasted_iota(jnp.int32, (8, LANES), 0)
    head = jnp.transpose(gram[0:LANES, :])[0:64, :]
    end = jnp.where(sub == 1, local_area, gram[LANES:FROWS, :])
    summed = jnp.concatenate([head, end], axis=0)
    copies = []
    first = 0
    for stride, size in stages_of(n):
        place = first + lax.rem(lax.div(me, stride), size)
        slots[place] = summed
        group = [
            pltpu.make_async_remote_copy(
                src_ref=slots.at[place],
                dst_ref=slots.at[place],
                send_sem=send_sem.at[first + step],
                recv_sem=recv_sem.at[first + step],
                device_id={"space": peer(stride, size, step)},
                device_id_type=mesh_type,
            )
            for step in range(1, size)
        ]
        for copy in group:
            copy.start()
        for copy in group:
            copy.wait_recv()
        summed = slots[first]
        for other in range(1, size):
            summed = summed + slots[first + other]
        copies += group
        first += size
    tail = summed[64:SLOT, :]
    per_area = 1.0 / tail[1:2, :]
    tail_t = jnp.transpose(jnp.concatenate([tail * per_area] * (LANES // 8), axis=0))
    summed = jnp.concatenate([summed[0:64, :] * per_area, tail_t[0:64, :]], axis=1)

    column = lax.broadcasted_iota(jnp.int32, (NBLK, 2 * LANES), 0)
    valid = lax.broadcasted_iota(jnp.int32, (NBLK, 2 * LANES), 1) < NFREQ
    a_re = []
    a_im = []
    for i in range(NBLK):
        unit = jnp.where(column == i, 1.0, 0.0)
        a_re.append(jnp.where(valid, summed[8 * i : 8 * i + 8, :], unit))
        part = summed[8 * (7 - i) : 8 * (7 - i) + 8, :]
        part = pltpu.roll(part, i + 1, 0) if i < NBLK - 1 else part
        a_im.append(jnp.where(valid & (column > i), part, 0.0))
    r_re = []
    r_im = []
    inv_diag = []
    for i in range(NBLK):
        scale = 1.0 / jnp.sqrt(a_re[i][i : i + 1, :])
        inv_diag.append(scale)
        r_re.append(jnp.where(column >= i, a_re[i] * scale, 0.0))
        r_im.append(jnp.where(column > i, a_im[i] * scale, 0.0))
        for k in range(i + 1, NBLK):
            c_re = r_re[i][k : k + 1, :]
            c_im = r_im[i][k : k + 1, :]
            a_re[k] = a_re[k] - (c_re * r_re[i] + c_im * r_im[i])
            a_im[k] = a_im[k] - (c_re * r_im[i] - c_im * r_re[i])
    x_re = [None] * NBLK
    x_im = [None] * NBLK
    for i in range(NBLK - 1, -1, -1):
        sum_re = jnp.where(column == i, 1.0, 0.0)
        sum_im = jnp.zeros((NBLK, 2 * LANES), jnp.float32)
        for m in range(i + 1, NBLK):
            c_re = r_re[i][m : m + 1, :]
            c_im = r_im[i][m : m + 1, :]
            sum_re = sum_re - (c_re * x_re[m] - c_im * x_im[m])
            sum_im = sum_im - (c_re * x_im[m] + c_im * x_re[m])
        x_re[i] = sum_re * inv_diag[i]
        x_im[i] = sum_im * inv_diag[i]

    def by_frequency(parts_re, parts_im):
        stacked = jnp.concatenate(parts_re + parts_im, axis=0)
        head = jnp.transpose(stacked[:, 0:LANES])
        end = jnp.transpose(stacked[:, LANES : 2 * LANES])
        return head, end[0:8, :]

    head, end = by_frequency(x_re, x_im)
    coef[0:LANES, :] = head
    coef[LANES:FROWS, :] = end
    for i, part in enumerate(r_re + r_im):
        factor_ref[i * NBLK : (i + 1) * NBLK, :] = part[:, 0:NFREQ]

    def mode_rows(first, count, store):
        re_rows = pl.ds(first, count)
        im_rows = pl.ds(FROWS + first, count)
        c = coef[re_rows, :]
        for l in range(NBLK):
            out_re = jnp.zeros((count, points), jnp.float32)
            out_im = jnp.zeros((count, points), jnp.float32)
            for k in range(l + 1):
                q_re = real[k, re_rows, :]
                q_im = real[k, im_rows, :]
                c_re = c[:, k * 8 + l : k * 8 + l + 1]
                out_re = out_re + q_re * c_re
                out_im = out_im + q_im * c_re
                if k < l:
                    c_im = c[:, 64 + k * 8 + l : 64 + k * 8 + l + 1]
                    out_re = out_re - q_im * c_im
                    out_im = out_im + q_re * c_im
            store(0, l, (out_re * live).astype(jnp.bfloat16))
            store(1, l, (out_im * live).astype(jnp.bfloat16))

    def mode_tile(tile, carry):
        first = pl.multiple_of(tile * 16, 16)

        def store(part, l, value):
            modes_ref[part, l, pl.ds(first, 16), :] = value

        mode_rows(first, 16, store)
        return carry

    lax.fori_loop(0, LANES // 16, mode_tile, 0)

    def store_tail(part, l, value):
        modes_ref[part, l, LANES:NFREQ, :] = value[0 : NFREQ - LANES, :]

    mode_rows(LANES, 8, store_tail)
    for copy in copies:
        copy.wait_send()

    def sent_block(turn, carry):
        block_copy(turn).wait_send()
        return carry

    lax.fori_loop(0, n - 1, sent_block, 0)


def per_device(snapshots, weights, counts, starts):
    n = lax.axis_size("space")
    rows, width = snapshots.shape
    points = width // n
    vmem = pl.BlockSpec(memory_space=pltpu.VMEM)
    smem = pl.BlockSpec(memory_space=pltpu.SMEM)
    slot_count = sum(size for stride, size in stages_of(n))
    anywhere = pl.BlockSpec(memory_space=pl.ANY)
    dma = pltpu.SemaphoreType.DMA
    modes, factor = pl.pallas_call(
        functools.partial(kernel, n),
        out_shape=(
            jax.ShapeDtypeStruct((2, NBLK, NFREQ, points), jnp.bfloat16),
            jax.ShapeDtypeStruct((2 * NBLK * NBLK, NFREQ), jnp.float32),
        ),
        in_specs=[smem, smem, vmem, anywhere, anywhere],
        out_specs=(vmem, vmem),
        scratch_shapes=[
            pltpu.VMEM((rows * n + 8, points), jnp.float32),
            pltpu.VMEM((8, 4 * FROWS, NFFT), jnp.bfloat16),
            pltpu.VMEM((NBLK, 2 * FROWS, points), jnp.float32),
            pltpu.VMEM((FROWS, LANES), jnp.float32),
            pltpu.VMEM((slot_count, SLOT, LANES), jnp.float32),
            pltpu.VMEM((FROWS, LANES), jnp.float32),
            dma((slot_count,)),
            dma((slot_count,)),
            dma,
            dma,
            dma((n,)),
            dma((n,)),
        ],
        compiler_params=pltpu.CompilerParams(
            collective_id=0, has_side_effects=True, vmem_limit_bytes=60 * 2**20
        ),
    )(starts, counts, weights[None, :], snapshots, jnp.asarray(window_table()))
    factor = factor.reshape(2, NBLK, NBLK, NFREQ)
    return (modes, jnp.moveaxis(factor, 3, 1))


def solution(mesh):
    in_specs = (P("space", "case"), P(("case", "space")), P(("case", "space")), P())
    out_specs = (P(None, None, None, ("case", "space")), P(None, "case", None, None))
    return jax.shard_map(
        per_device, mesh=mesh, in_specs=in_specs, out_specs=out_specs, check_vma=False
    )
```

```python
import functools

import jax
import jax.numpy as jnp
import numpy as np
from jax import lax
from jax.experimental import pallas as pl
from jax.experimental.pallas import tpu as pltpu
from jax.sharding import PartitionSpec as P

NFFT = 256
NBLK = 8
NFREQ = NFFT // 2 + 1
FROWS = 136
LANES = 128
SLOT = 72


def window_table():
    moment = np.arange(NFFT)
    harmonic = np.arange(NFREQ)
    hann = 0.5 - 0.5 * np.cos(2.0 * np.pi * moment / NFFT)
    scale = 1.0 / np.sqrt(np.sum(hann * hann))
    angle = 2.0 * np.pi * (harmonic[:, None] * moment[None, :] % NFFT) / NFFT
    table = np.zeros((2 * FROWS, NFFT))
    table[:NFREQ] = np.cos(angle) * hann * scale
    table[FROWS : FROWS + NFREQ] = -np.sin(angle) * hann * scale
    table = table.astype(np.float32)
    high = table.astype(jnp.bfloat16)
    low = (table - high.astype(np.float32)).astype(jnp.bfloat16)
    both = np.concatenate([high, low], axis=0)
    return np.stack([np.roll(both, turn, axis=1) for turn in range(8)])


def stages_of(n):
    return [(1, 2), (2, 2), (4, n // 4)]


def kernel(
    n,
    starts_ref,
    counts_ref,
    weights_ref,
    snap_ref,
    table_hbm,
    modes_ref,
    factor_ref,
    rec,
    table,
    real,
    gram,
    slots,
    coef,
    send_sem,
    recv_sem,
    own_sem,
    table_sem,
    block_send,
    block_recv,
):
    me = lax.axis_index("space")
    rows = snap_ref.shape[0]
    points = snap_ref.shape[1] // n
    record_rows = rows * n
    mesh_type = pl.DeviceIdType.MESH

    def peer(stride, size, step):
        place = lax.rem(lax.div(me, stride), size)
        return me + (lax.rem(place + step, size) - place) * stride

    barrier = pltpu.get_barrier_semaphore()

    def greet(step, carry):
        pl.semaphore_signal(
            barrier,
            inc=1,
            device_id={"space": lax.rem(me + step, n)},
            device_id_type=mesh_type,
        )
        return carry

    lax.fori_loop(1, n, greet, 0)

    def rows_of(shard):
        return pl.ds(pl.multiple_of(shard * rows, 8), rows)

    def columns(shard):
        return pl.ds(pl.multiple_of(shard * points, LANES), points)

    def block_copy(turn):
        step = 1 + lax.rem(turn + n // 2 - 1, n - 1)
        dest = lax.rem(me + step, n)
        return pltpu.make_async_remote_copy(
            src_ref=snap_ref.at[:, columns(dest)],
            dst_ref=rec.at[rows_of(me), :],
            send_sem=block_send.at[step],
            recv_sem=block_recv.at[step],
            device_id={"space": dest},
            device_id_type=mesh_type,
        )

    own = pltpu.make_async_copy(snap_ref.at[:, columns(me)], rec.at[rows_of(me), :], own_sem)
    fetch = pltpu.make_async_copy(table_hbm, table, table_sem)
    pl.semaphore_wait(barrier, n - 1)

    def send_block(turn, carry):
        block_copy(turn).start()
        return carry

    lax.fori_loop(0, n - 1, send_block, 0)
    own.start()
    fetch.start()
    live = (lax.broadcasted_iota(jnp.int32, (1, points), 1) < counts_ref[0]).astype(jnp.float32)
    area = weights_ref[...] * live

    own.wait()

    def take_block(turn, total):
        step = 1 + turn
        pltpu.make_async_remote_copy(
            src_ref=snap_ref.at[:, columns(me)],
            dst_ref=rec.at[rows_of(me), :],
            send_sem=block_send.at[step],
            recv_sem=block_recv.at[step],
            device_id={"space": lax.rem(me + step, n)},
            device_id_type=mesh_type,
        ).wait_recv()
        return total + rec[rows_of(lax.rem(me + n - step, n)), :]

    sums = lax.fori_loop(0, n - 1, take_block, rec[rows_of(me), :])
    mean = jnp.sum(sums, axis=0, keepdims=True) * (1.0 / record_rows)
    rec[record_rows : record_rows + 8, :] = jnp.zeros((8, points), jnp.float32)
    fetch.wait()

    early = lax.broadcasted_iota(jnp.int32, (8, points), 0)

    def transform(block, carry):
        start = starts_ref[block]
        base = lax.div(start, 8) * 8
        shift = start - base
        wrapped = jnp.where(early < shift, rec[pl.ds(base + NFFT, 8), :], rec[pl.ds(base, 8), :])
        segment = jnp.concatenate([wrapped, rec[pl.ds(base + 8, NFFT - 8), :]], axis=0) - mean
        seg_high = segment.astype(jnp.bfloat16)
        seg_low = (segment - seg_high.astype(jnp.float32)).astype(jnp.bfloat16)
        high = table[shift, 0 : 2 * FROWS, :]
        low = table[shift, 2 * FROWS : 4 * FROWS, :]
        dot = functools.partial(jnp.dot, preferred_element_type=jnp.float32)
        real[block] = dot(high, seg_high) + (dot(high, seg_low) + dot(low, seg_high))
        return carry

    lax.fori_loop(0, NBLK, transform, 0, unroll=4)

    lane = lax.broadcasted_iota(jnp.int32, (8, LANES), 1)

    def gram_tile(tile, carry):
        re_rows = pl.ds(pl.multiple_of(tile * 8, 8), 8)
        im_rows = pl.ds(pl.multiple_of(FROWS + tile * 8, 8), 8)
        packed = jnp.zeros((8, LANES), jnp.float32)
        q_re = [real[k, re_rows, :] for k in range(NBLK)]
        q_im = [real[k, im_rows, :] for k in range(NBLK)]
        for k in range(NBLK):
            w_re = q_re[k] * area
            w_im = q_im[k] * area
            for l in range(k, NBLK):
                entry = jnp.sum(w_re * q_re[l] + w_im * q_im[l], axis=1, keepdims=True)
                packed = jnp.where(lane == k * 8 + l, entry, packed)
                if l > k:
                    entry = jnp.sum(w_re * q_im[l] - w_im * q_re[l], axis=1, keepdims=True)
                    packed = jnp.where(lane == (7 - k) * 8 + l - k - 1, entry, packed)
        gram[re_rows, :] = packed
        return carry

    lax.fori_loop(0, FROWS // 8, gram_tile, 0)
    local_area = jnp.sum(area, axis=1, keepdims=True)
    sub = lax.broadcasted_iota(jnp.int32, (8, LANES), 0)
    head = jnp.transpose(gram[0:LANES, :])[0:64, :]
    end = jnp.where(sub == 1, local_area, gram[LANES:FROWS, :])
    summed = jnp.concatenate([head, end], axis=0)
    copies = []
    first = 0
    for stride, size in stages_of(n):
        place = first + lax.rem(lax.div(me, stride), size)
        slots[place] = summed
        group = [
            pltpu.make_async_remote_copy(
                src_ref=slots.at[place],
                dst_ref=slots.at[place],
                send_sem=send_sem.at[first + step],
                recv_sem=recv_sem.at[first + step],
                device_id={"space": peer(stride, size, step)},
                device_id_type=mesh_type,
            )
            for step in range(1, size)
        ]
        for copy in group:
            copy.start()
        for copy in group:
            copy.wait_recv()
        summed = slots[first]
        for other in range(1, size):
            summed = summed + slots[first + other]
        copies += group
        first += size
    tail = summed[64:SLOT, :]
    per_area = 1.0 / tail[1:2, :]
    tail_t = jnp.transpose(jnp.concatenate([tail * per_area] * (LANES // 8), axis=0))
    summed = jnp.concatenate([summed[0:64, :] * per_area, tail_t[0:64, :]], axis=1)

    column = lax.broadcasted_iota(jnp.int32, (NBLK, 2 * LANES), 0)
    valid = lax.broadcasted_iota(jnp.int32, (NBLK, 2 * LANES), 1) < NFREQ
    a_re = []
    a_im = []
    for i in range(NBLK):
        unit = jnp.where(column == i, 1.0, 0.0)
        a_re.append(jnp.where(valid, summed[8 * i : 8 * i + 8, :], unit))
        part = summed[8 * (7 - i) : 8 * (7 - i) + 8, :]
        part = pltpu.roll(part, i + 1, 0) if i < NBLK - 1 else part
        a_im.append(jnp.where(valid & (column > i), part, 0.0))
    r_re = []
    r_im = []
    inv_diag = []
    for i in range(NBLK):
        scale = 1.0 / jnp.sqrt(a_re[i][i : i + 1, :])
        inv_diag.append(scale)
        r_re.append(jnp.where(column >= i, a_re[i] * scale, 0.0))
        r_im.append(jnp.where(column > i, a_im[i] * scale, 0.0))
        for k in range(i + 1, NBLK):
            c_re = r_re[i][k : k + 1, :]
            c_im = r_im[i][k : k + 1, :]
            a_re[k] = a_re[k] - (c_re * r_re[i] + c_im * r_im[i])
            a_im[k] = a_im[k] - (c_re * r_im[i] - c_im * r_re[i])
    x_re = [None] * NBLK
    x_im = [None] * NBLK
    for i in range(NBLK - 1, -1, -1):
        sum_re = jnp.where(column == i, 1.0, 0.0)
        sum_im = jnp.zeros((NBLK, 2 * LANES), jnp.float32)
        for m in range(i + 1, NBLK):
            c_re = r_re[i][m : m + 1, :]
            c_im = r_im[i][m : m + 1, :]
            sum_re = sum_re - (c_re * x_re[m] - c_im * x_im[m])
            sum_im = sum_im - (c_re * x_im[m] + c_im * x_re[m])
        x_re[i] = sum_re * inv_diag[i]
        x_im[i] = sum_im * inv_diag[i]

    def by_frequency(parts_re, parts_im):
        stacked = jnp.concatenate(parts_re + parts_im, axis=0)
        head = jnp.transpose(stacked[:, 0:LANES])
        end = jnp.transpose(stacked[:, LANES : 2 * LANES])
        return head, end[0:8, :]

    head, end = by_frequency(x_re, x_im)
    coef[0:LANES, :] = head
    coef[LANES:FROWS, :] = end
    for i, part in enumerate(r_re + r_im):
        factor_ref[i * NBLK : (i + 1) * NBLK, :] = part[:, 0:NFREQ]

    def mode_rows(first, count, store):
        re_rows = pl.ds(first, count)
        im_rows = pl.ds(FROWS + first, count)
        c = coef[re_rows, :]
        for l in range(NBLK):
            out_re = jnp.zeros((count, points), jnp.float32)
            out_im = jnp.zeros((count, points), jnp.float32)
            for k in range(l + 1):
                q_re = real[k, re_rows, :]
                q_im = real[k, im_rows, :]
                c_re = c[:, k * 8 + l : k * 8 + l + 1]
                out_re = out_re + q_re * c_re
                out_im = out_im + q_im * c_re
                if k < l:
                    c_im = c[:, 64 + k * 8 + l : 64 + k * 8 + l + 1]
                    out_re = out_re - q_im * c_im
                    out_im = out_im + q_re * c_im
            store(0, l, (out_re * live).astype(jnp.bfloat16))
            store(1, l, (out_im * live).astype(jnp.bfloat16))

    def mode_tile(tile, carry):
        first = pl.multiple_of(tile * 16, 16)

        def store(part, l, value):
            modes_ref[part, l, pl.ds(first, 16), :] = value

        mode_rows(first, 16, store)
        return carry

    lax.fori_loop(0, LANES // 16, mode_tile, 0)

    def store_tail(part, l, value):
        modes_ref[part, l, LANES:NFREQ, :] = value[0 : NFREQ - LANES, :]

    mode_rows(LANES, 8, store_tail)
    for copy in copies:
        copy.wait_send()

    def sent_block(turn, carry):
        block_copy(turn).wait_send()
        return carry

    lax.fori_loop(0, n - 1, sent_block, 0)


def per_device(snapshots, weights, counts, starts):
    n = lax.axis_size("space")
    rows, width = snapshots.shape
    points = width // n
    vmem = pl.BlockSpec(memory_space=pltpu.VMEM)
    smem = pl.BlockSpec(memory_space=pltpu.SMEM)
    slot_count = sum(size for stride, size in stages_of(n))
    anywhere = pl.BlockSpec(memory_space=pl.ANY)
    dma = pltpu.SemaphoreType.DMA
    modes, factor = pl.pallas_call(
        functools.partial(kernel, n),
        out_shape=(
            jax.ShapeDtypeStruct((2, NBLK, NFREQ, points), jnp.bfloat16),
            jax.ShapeDtypeStruct((2 * NBLK * NBLK, NFREQ), jnp.float32),
        ),
        in_specs=[smem, smem, vmem, anywhere, anywhere],
        out_specs=(vmem, vmem),
        scratch_shapes=[
            pltpu.VMEM((rows * n + 8, points), jnp.float32),
            pltpu.VMEM((8, 4 * FROWS, NFFT), jnp.bfloat16),
            pltpu.VMEM((NBLK, 2 * FROWS, points), jnp.float32),
            pltpu.VMEM((FROWS, LANES), jnp.float32),
            pltpu.VMEM((slot_count, SLOT, LANES), jnp.float32),
            pltpu.VMEM((FROWS, LANES), jnp.float32),
            dma((slot_count,)),
            dma((slot_count,)),
            dma,
            dma,
            dma((n,)),
            dma((n,)),
        ],
        compiler_params=pltpu.CompilerParams(
            collective_id=0, has_side_effects=True, vmem_limit_bytes=60 * 2**20
        ),
    )(starts, counts, weights[None, :], snapshots, jnp.asarray(window_table()))
    factor = factor.reshape(2, NBLK, NBLK, NFREQ)
    return (modes, jnp.moveaxis(factor, 3, 1))


def solution(mesh):
    in_specs = (P("space", "case"), P(("case", "space")), P(("case", "space")), P())
    out_specs = (P(None, None, None, ("case", "space")), P(None, "case", None, None))
    return jax.shard_map(
        per_device, mesh=mesh, in_specs=in_specs, out_specs=out_specs, check_vma=False
    )
```
